512 devices in a mesh: dp: 16 (over z, x_hi), seq: 32 (over x_lo, y, core).
Axes of the slice: x: 4 (x_hi: 2, x_lo: 2; x = x_hi * 2 + x_lo), y: 8, z: 8, core: 2. Of those that a mesh axis runs over, the one named last changes fastest.
Arguments:
- queries: bfloat16 [65536, 1792], P(('dp', 'seq')), may hold values from -64 to 64
- keys: bfloat16 [65536, 256], P(('dp', 'seq')), may hold values from -3 to 3
- values: bfloat16 [65536, 256], P(('dp', 'seq')), may hold values from -6 to 6
- bias_query: bfloat16 [1792], replicated, may hold values from -3 to 3
- bias_value: bfloat16 [256], replicated, may hold values from -3 to 3
- doc_lengths: int32 [16, 16], P('dp'), may hold values from 1 to 3072, 4096 in all within a row
- grad_out: bfloat16 [65536, 1792], P(('dp', 'seq')), may hold values from -24 to 24
Outputs:
- attended: bfloat16 [65536, 1792], P(('dp', 'seq'))
- grad_queries: bfloat16 [65536, 1792], P(('dp', 'seq'))
- grad_keys: bfloat16 [65536, 256], P(('dp', 'seq'))
- grad_values: bfloat16 [65536, 256], P(('dp', 'seq'))
- grad_bias_query: float32 [1792], replicated
- grad_bias_value: float32 [256], replicated
The draws below stay inside these ranges and needn't reach their ends.
Inputs may be any that keep to these rules, and one draw needn't show every extreme that they name: `doc_lengths`: the 16 lengths of each pack add up to 4096, and the longest is 3072.
All inputs are finite; a program needn't handle non-finite values.
Results may differ from the reference program's by a relative error of at most 0.023.
Values may be sent and summed in bfloat16 or wider, within the bound.
No kernel may reach another device: no remote copies, remote signals or barrier semaphores. Data moves between devices by JAX's collectives and lax.ppermute only.
A program may use at most 64 MiB of HBM per device.

```python
import math
import jax
import jax.numpy as jnp
import numpy as np
from jax import lax

HEADS = 14
KV_HEADS = 2
HEAD_DIM = 128
TOK_DEV = 128
NDOC = 16
GTOK = 4096
LONGEST = 3072
TOKENS = 65536
N_DP = 16
N_SEQ = 32


def shared_base(key):
    raw = jax.random.normal(key, (TOKENS, KV_HEADS * HEAD_DIM), jnp.float32)
    return jnp.clip(raw, -3.0, 3.0)


def spread_heads(rows):
    return jnp.broadcast_to(rows.reshape(TOKENS, KV_HEADS, 1, HEAD_DIM), (TOKENS, KV_HEADS, HEADS // KV_HEADS, HEAD_DIM)).reshape(TOKENS, HEADS * HEAD_DIM)


def draw_keys(key, part):
    base = shared_base(key)
    return base.astype(jnp.bfloat16)


def draw_queries(key, part):
    base = shared_base(key)
    key = jax.random.fold_in(key, 7)
    fresh = jnp.clip(jax.random.normal(key, (TOKENS, HEADS * HEAD_DIM), jnp.float32), -4.0, 4.0)
    distance = GTOK // 2 - TOK_DEV // 2
    far_distance = LONGEST - TOK_DEV // 2
    fresh = fresh + 0.8 * spread_heads(jnp.roll(base, distance, axis=0))
    fresh = fresh + 1.5 * spread_heads(jnp.roll(base, far_distance, axis=0))
    return fresh.astype(jnp.bfloat16)


def strengthened(drawn, stream_key, source, target, parts, factor):
    def block_of(position):
        return (jnp.arange(drawn.shape[position]) // (drawn.shape[position] // parts)).reshape((-1,) + (1,) * (drawn.ndim - 1 - position))

    one_side = jax.random.permutation(stream_key, parts)[block_of(target)]
    second = (block_of(target) + parts // 2) % parts
    return jnp.where((block_of(source) == one_side) | (block_of(source) == second), factor * drawn, drawn)


def block_scale(rng, extent, shards, low, high):
    factor_of, own = 1.0, jax.random.fold_in(rng, 6)
    for dim, parts in shards:
        steps = jnp.exp(jax.random.uniform(jax.random.fold_in(own, dim), (parts,), jnp.float32, low / len(shards), high / len(shards)))
        factor_of = factor_of * jnp.repeat(steps, extent[dim] // parts).reshape([-1 if axis == dim else 1 for axis in range(len(extent))])
    return factor_of


def profile(amount, total, reach, lean):
    portions = [(1 << 20) // math.isqrt(standing ** lean) + 1 for standing in range(2, amount + 1)]
    surplus, holding = total - reach - (amount - 1), [1] * (amount - 1)
    while surplus > 0:
        movable = [i for i in range(amount - 1) if holding[i] < reach]
        whole, budget = sum([portions[i] for i in movable]), surplus
        for i in movable:
            more = min(reach - holding[i], max(1, budget * portions[i] // whole), surplus)
            holding[i] = holding[i] + more
            surplus = surplus - more
    return np.array([reach] + holding)


def ragged(rng, number_of, total, limit, lean):
    if number_of == 2:
        one = jax.random.randint(rng, (), max(1, total - limit), min(limit, total - 1) + 1)
        return jnp.stack([one, total - one])
    lengths = jnp.asarray(profile(number_of, total, limit, lean), jnp.int32)
    twos = (number_of - 1) // 2
    giver, taker = lengths[1:1 + 2 * twos:2], lengths[2:2 + 2 * twos:2]
    slack = jnp.minimum(giver - 1, limit - taker)
    passed = jax.random.randint(jax.random.fold_in(rng, 1), (twos,), 0, 1 << 20) % (slack + 1)
    lengths = lengths.at[1:1 + 2 * twos:2].set(giver - passed).at[2:2 + 2 * twos:2].set(taker + passed)
    return lengths[jax.random.permutation(jax.random.fold_in(rng, 2), number_of)]


def normal_values(own_key, dims, scale, limit, shards=(), kind=jnp.bfloat16):
    drawn = jax.random.normal(own_key, dims, jnp.float32) * scale
    if len(shards) > 0:
        drawn = block_scale(own_key, dims, shards, -0.22, 0.18) * drawn
    return jnp.clip(drawn, min=-limit, max=limit).astype(kind)


def noise_with(rng, shape, scale, most, cuts, heavy, kind=jnp.bfloat16):
    result = scale * jax.random.normal(rng, shape, jnp.float32)
    if cuts:
        result = result * block_scale(rng, shape, cuts, -0.22, 0.18)
    return jnp.clip(strengthened(result, jax.random.fold_in(rng, 3), *heavy), -most, most).astype(kind)


def setup_inputs(seed: int = 0) -> dict:
    seeds = jax.random.split(jax.random.key(seed), 8)
    return {
        "queries": draw_queries(jax.random.fold_in(seeds[7], 71), 0),
        "keys": draw_keys(jax.random.fold_in(seeds[7], 71), 0),
        "values": normal_values(seeds[2], (TOKENS, KV_HEADS * HEAD_DIM), 1.0, 6.0, ((0, 512),)),
        "bias_query": normal_values(seeds[3], (HEADS * HEAD_DIM,), 0.5, 3.0),
        "bias_value": normal_values(seeds[4], (KV_HEADS * HEAD_DIM,), 0.5, 3.0),
        "doc_lengths": jax.vmap(lambda own: ragged(own, NDOC, GTOK, LONGEST, 2))(jax.random.split(seeds[5], N_DP)).reshape((N_DP, NDOC)).astype(jnp.int32),
        "grad_out": noise_with(seeds[6], (TOKENS, HEADS * HEAD_DIM), 1.0, 24.0, ((0, 512),), (0, 1, 256, 6.0)),
    }


NEGATIVE = -1e+30

def doc_starts(doc_lengths, token_index):
    lengths_row = doc_lengths.reshape(-1).astype(jnp.int32)
    ends = jnp.cumsum(lengths_row).astype(jnp.int32)
    begins = (ends - lengths_row).astype(jnp.int32)
    below = begins[None, :] <= token_index[:, None]
    return lax.optimization_barrier(jnp.max(jnp.where(below, begins[None, :], 0), axis=1)).astype(jnp.int32)

def round_keep(tensor):
    return lax.optimization_barrier(tensor.astype(jnp.bfloat16)).astype(jnp.float32)

def reference(queries, keys, values, bias_query, bias_value, doc_lengths, grad_out):
    group_q = HEADS // KV_HEADS
    scale = 1.0 / math.sqrt(HEAD_DIM)
    query_block = TOK_DEV * min(N_SEQ, max(1, 512 // TOK_DEV))
    shard_count = query_block // TOK_DEV
    query_rows = (queries.astype(jnp.float32) + bias_query.astype(jnp.float32)[None, :]).astype(jnp.bfloat16)
    value_rows = (values.astype(jnp.float32) + bias_value.astype(jnp.float32)[None, :]).astype(jnp.bfloat16)

    def one_group(packed):
        q_all, k_all, v_all, g_all, lens = packed
        token_index = jnp.arange(GTOK, dtype=jnp.int32)
        first_seen = doc_starts(lens, token_index)
        outputs = []
        query_grads = []
        key_sum = jnp.zeros((GTOK, KV_HEADS * HEAD_DIM), jnp.float32)
        value_sum = jnp.zeros((GTOK, KV_HEADS * HEAD_DIM), jnp.float32)
        bias_part = jnp.zeros((HEADS * HEAD_DIM,), jnp.float32)
        for block in range(GTOK // query_block):
            low = block * query_block
            high = low + query_block
            q_grp = q_all[low:high].reshape(query_block, KV_HEADS, group_q, HEAD_DIM).astype(jnp.float32)
            g_grp = g_all[low:high].reshape(query_block, KV_HEADS, group_q, HEAD_DIM).astype(jnp.float32)
            k_heads = k_all[:high].reshape(high, KV_HEADS, HEAD_DIM).astype(jnp.float32)
            v_heads = v_all[:high].reshape(high, KV_HEADS, HEAD_DIM).astype(jnp.float32)
            raw = jnp.einsum('tkgd,skd->kgts', q_grp, k_heads) * scale
            key_index = jnp.arange(high, dtype=jnp.int32)
            query_index = token_index[low:high]
            allowed = jnp.logical_and(key_index[None, :] <= query_index[:, None], key_index[None, :] >= first_seen[low:high][:, None])
            masked = jnp.where(allowed[None, None], raw, NEGATIVE)
            best = lax.optimization_barrier(jnp.max(masked, axis=-1))
            totals = lax.optimization_barrier(jnp.sum(jnp.where(allowed[None, None], jnp.exp(masked - best[..., None]), 0.0), axis=-1))
            log_total = best + jnp.log(totals)
            probs = jnp.where(allowed[None, None], jnp.exp(raw - log_total[..., None]), 0.0)
            rounded = round_keep(probs)
            out_block = jnp.einsum('kgts,skd->tkgd', rounded, v_heads).astype(jnp.bfloat16)
            delta = lax.optimization_barrier(jnp.sum(g_grp * out_block.astype(jnp.float32), axis=-1)).transpose(1, 2, 0)
            dots = jnp.einsum('tkgd,skd->kgts', g_grp, v_heads)
            slopes = round_keep(probs * (dots - delta[..., None]))
            query_grad = jnp.einsum('kgts,skd->tkgd', slopes, k_heads).reshape(query_block, HEADS * HEAD_DIM) * scale
            outputs.append(out_block.reshape(query_block, HEADS * HEAD_DIM))
            query_grads.append(query_grad.astype(jnp.bfloat16))
            bias_part = bias_part + lax.optimization_barrier(jnp.sum(query_grad, axis=0))
            slopes_split = slopes.reshape(KV_HEADS, group_q, shard_count, TOK_DEV, high)
            rounded_split = rounded.reshape(KV_HEADS, group_q, shard_count, TOK_DEV, high)
            q_split = q_grp.reshape(shard_count, TOK_DEV, KV_HEADS, group_q, HEAD_DIM)
            g_split = g_grp.reshape(shard_count, TOK_DEV, KV_HEADS, group_q, HEAD_DIM)
            key_parts = round_keep(jnp.einsum('kgjts,jtkgd->jskd', slopes_split, q_split) * scale)
            value_parts = round_keep(jnp.einsum('kgjts,jtkgd->jskd', rounded_split, g_split))
            key_sum = key_sum.at[:high].add(lax.optimization_barrier(jnp.sum(key_parts, axis=0)).reshape(high, KV_HEADS * HEAD_DIM))
            value_sum = value_sum.at[:high].add(lax.optimization_barrier(jnp.sum(value_parts, axis=0)).reshape(high, KV_HEADS * HEAD_DIM))
        return (jnp.concatenate(outputs, axis=0), jnp.concatenate(query_grads, axis=0), key_sum, value_sum, bias_part)
    packed = (query_rows.reshape(N_DP, GTOK, HEADS * HEAD_DIM), keys.reshape(N_DP, GTOK, KV_HEADS * HEAD_DIM), value_rows.reshape(N_DP, GTOK, KV_HEADS * HEAD_DIM), grad_out.reshape(N_DP, GTOK, HEADS * HEAD_DIM), doc_lengths.astype(jnp.int32))
    attended, grad_q, key_sum, value_sum, bias_parts = lax.map(one_group, packed)
    grad_bias_query = lax.optimization_barrier(jnp.sum(bias_parts, axis=0))
    grad_bias_value = lax.optimization_barrier(jnp.sum(value_sum.reshape(TOKENS, KV_HEADS * HEAD_DIM), axis=0))
    return (attended.reshape(TOKENS, HEADS * HEAD_DIM), grad_q.reshape(TOKENS, HEADS * HEAD_DIM), key_sum.reshape(TOKENS, KV_HEADS * HEAD_DIM).astype(jnp.bfloat16), value_sum.reshape(TOKENS, KV_HEADS * HEAD_DIM).astype(jnp.bfloat16), grad_bias_query, grad_bias_value)
```

```python
import functools
import math

import jax
import jax.numpy as jnp
from jax import lax
from jax.experimental import pallas as pl
from jax.experimental.pallas import tpu as pltpu
from jax.sharding import Mesh, PartitionSpec as P

HEADS = 14
KV_HEADS = 2
HEAD_DIM = 128
GROUP = HEADS // KV_HEADS
TOK = 128
CHUNK = 256
LONGEST = 3072
SLOTS = LONGEST // CHUNK + 1
NDOC = 16
SCALE = 1.0 / math.sqrt(HEAD_DIM)
LOG2E = math.log2(math.e)
NEGATIVE = -1e30
F32 = jnp.float32
BF16 = jnp.bfloat16


def dot(a, b):
    return jnp.dot(a, b, preferred_element_type=F32)


def fold_rows(values, how):
    return how(values.reshape(values.shape[0] // 8, 8, values.shape[1]), axis=0)


def attention_kernel(
    place, lengths, q_own, g_own, q_other, g_other, bias, kv,
    att_own, att_send, gq_own, gq_send, dkv, bias_out,
    q_s, qt_s, g_s, gt_s, s_s, mx_s, l_s, ot_s, dqt_s, rl_s, delta_s, mask_s, bv_s,
):
    core = place[0]
    chunk_id = place[1]
    first_token = chunk_id * CHUNK

    token = first_token + lax.broadcasted_iota(jnp.int32, (1, CHUNK), 1)
    first_seen = jnp.zeros((1, CHUNK), jnp.int32)
    begin = jnp.int32(0)
    lowest = jnp.int32(0)
    for i in range(NDOC):
        first_seen = jnp.where(token >= begin, begin, first_seen)
        lowest = jnp.where(first_token >= begin, begin, lowest)
        begin = begin + lengths[0, i]
    low = lax.div(lowest, jnp.int32(CHUNK))

    own_at = pl.multiple_of(core * TOK, TOK)
    other_at = pl.multiple_of((1 - core) * TOK, TOK)
    for h in range(GROUP):
        cols = pl.ds(h * HEAD_DIM, HEAD_DIM)
        own_cols = pl.ds(pl.multiple_of((core * GROUP + h) * HEAD_DIM, HEAD_DIM), HEAD_DIM)
        bias_row = bias[:, own_cols].astype(F32)
        q_s[h, pl.ds(own_at, TOK), :] = (q_own[:, own_cols].astype(F32) + bias_row).astype(BF16)
        q_s[h, pl.ds(other_at, TOK), :] = (q_other[:, cols].astype(F32) + bias_row).astype(BF16)
        g_s[h, pl.ds(own_at, TOK), :] = g_own[:, own_cols]
        g_s[h, pl.ds(other_at, TOK), :] = g_other[:, cols]
    for h in range(GROUP):
        qt_s[h] = q_s[h].T
        gt_s[h] = g_s[h].T
    mx_s[...] = jnp.full(mx_s.shape, NEGATIVE, F32)
    l_s[...] = jnp.zeros(l_s.shape, F32)
    ot_s[...] = jnp.zeros(ot_s.shape, F32)
    dqt_s[...] = jnp.zeros(dqt_s.shape, F32)
    bv_s[...] = jnp.zeros(bv_s.shape, F32)
    dkv[...] = jnp.zeros(dkv.shape, BF16)

    def where_of(c):
        return lax.rem(c, 8), lax.div(c, 8)

    def scores(c, carry):
        y, x = where_of(c)
        keys = kv[y, x, :, :HEAD_DIM]
        key_index = c * CHUNK + lax.broadcasted_iota(jnp.int32, (CHUNK, CHUNK), 0)
        allowed = jnp.logical_and(key_index <= token, key_index >= first_seen)
        mask_s[...] = jnp.where(allowed, 0.0, NEGATIVE)
        for h in range(GROUP):
            raw = dot(keys, qt_s[h]) * (SCALE * LOG2E) + mask_s[...]
            s_s[c - low, h] = raw
            mx_s[h] = jnp.maximum(mx_s[h], fold_rows(raw, jnp.max))
        return carry

    lax.fori_loop(low, chunk_id + 1, scores, 0)
    for h in range(GROUP):
        mx_s[h] = jnp.broadcast_to(jnp.max(mx_s[h], axis=0, keepdims=True), (8, CHUNK))

    def weigh(c, carry):
        y, x = where_of(c)
        values_t = kv[y, x, :, HEAD_DIM:].T
        for h in range(GROUP):
            probs = jnp.exp2(s_s[c - low, h] - mx_s[h, 0:1, :])
            s_s[c - low, h] = probs
            l_s[h] = l_s[h] + fold_rows(probs, jnp.sum)
            ot_s[h] = ot_s[h] + dot(values_t, probs.astype(BF16))
        return carry

    lax.fori_loop(low, chunk_id + 1, weigh, 0)

    for h in range(GROUP):
        cols = pl.ds(h * HEAD_DIM, HEAD_DIM)
        inverse = 1.0 / jnp.sum(l_s[h], axis=0, keepdims=True)
        rl_s[h] = jnp.broadcast_to(inverse, (8, CHUNK))
        out_t = (ot_s[h] * inverse).astype(BF16).astype(F32)
        delta = jnp.sum(out_t * gt_s[h].astype(F32), axis=0, keepdims=True)
        delta_s[h] = jnp.broadcast_to(delta, (8, CHUNK))
        ot_s[h] = out_t
        mx_s[h, :, :] = jnp.zeros((8, CHUNK), F32)
        out = out_t.T.astype(BF16)
        g_s_rows = out.reshape(2, TOK, HEAD_DIM)
        att_own[:, cols] = jnp.where(core == 0, g_s_rows[0], g_s_rows[1])
        att_send[:, cols] = jnp.where(core == 0, g_s_rows[1], g_s_rows[0])

    def slopes_of(c, carry):
        y, x = where_of(c)
        keys_t = kv[y, x, :, :HEAD_DIM].T
        values = kv[y, x, :, HEAD_DIM:]
        dk = jnp.zeros((CHUNK, HEAD_DIM), F32)
        dv = jnp.zeros((CHUNK, HEAD_DIM), F32)
        for h in range(GROUP):
            dots = dot(values, gt_s[h])
            probs = s_s[c - low, h] * rl_s[h, 0:1, :]
            slopes = (probs * (dots - delta_s[h, 0:1, :])).astype(BF16)
            dk = dk + dot(slopes, q_s[h])
            dv = dv + dot(probs.astype(BF16), g_s[h])
            dqt_s[h] = dqt_s[h] + dot(keys_t, slopes)
        dkv[y, x, :, :HEAD_DIM] = (dk * SCALE).astype(BF16)
        dkv[y, x, :, HEAD_DIM:] = dv.astype(BF16)
        bv_s[...] = bv_s[...] + fold_rows(dv, jnp.sum)
        return carry

    lax.fori_loop(low, chunk_id + 1, slopes_of, 0)

    for h in range(GROUP):
        cols = pl.ds(h * HEAD_DIM, HEAD_DIM)
        grad = (dqt_s[h] * SCALE).T
        bias_out[h : h + 1, :] = jnp.sum(grad, axis=0, keepdims=True)
        rows = grad.astype(BF16).reshape(2, TOK, HEAD_DIM)
        gq_own[:, cols] = jnp.where(core == 0, rows[0], rows[1])
        gq_send[:, cols] = jnp.where(core == 0, rows[1], rows[0])
    bias_out[GROUP : GROUP + 1, :] = jnp.sum(bv_s[...], axis=0, keepdims=True)


def attention(place, lengths, q_own, g_own, q_other, g_other, bias, kv):
    half = jax.ShapeDtypeStruct((TOK, GROUP * HEAD_DIM), BF16)
    vmem = pl.BlockSpec(memory_space=pltpu.VMEM)
    smem = pl.BlockSpec(memory_space=pltpu.SMEM)
    head = (GROUP, CHUNK, HEAD_DIM)
    head_t = (GROUP, HEAD_DIM, CHUNK)
    stat = (GROUP, 8, CHUNK)
    pairs = CHUNK * SLOTS * CHUNK * GROUP
    return pl.pallas_call(
        attention_kernel,
        out_shape=[half] * 4
        + [
            jax.ShapeDtypeStruct(kv.shape, BF16),
            jax.ShapeDtypeStruct((8, HEAD_DIM), F32),
        ],
        in_specs=[smem] * 2 + [vmem] * 6,
        out_specs=[vmem] * 6,
        scratch_shapes=[
            pltpu.VMEM(head, BF16),
            pltpu.VMEM(head_t, BF16),
            pltpu.VMEM(head, BF16),
            pltpu.VMEM(head_t, BF16),
            pltpu.VMEM((SLOTS, GROUP, CHUNK, CHUNK), F32),
            pltpu.VMEM(stat, F32),
            pltpu.VMEM(stat, F32),
            pltpu.VMEM(head_t, F32),
            pltpu.VMEM(head_t, F32),
            pltpu.VMEM(stat, F32),
            pltpu.VMEM(stat, F32),
            pltpu.VMEM((CHUNK, CHUNK), F32),
            pltpu.VMEM((8, HEAD_DIM), F32),
        ],
        compiler_params=pltpu.CompilerParams(vmem_limit_bytes=58 * 1024 * 1024),
        cost_estimate=pl.CostEstimate(
            flops=12 * pairs * HEAD_DIM, bytes_accessed=8 << 20, transcendentals=pairs
        ),
    )(place, lengths, q_own, g_own, q_other, g_other, bias, kv)


SEQ = ("xlo", "y", "core")
SWAP = [(0, 1), (1, 0)]


def everyone(part, axes, count):
    spread = jnp.broadcast_to(part[None], (count,) + part.shape)
    return lax.all_to_all(spread, axes, split_axis=0, concat_axis=0, tiled=True)


def body(queries, keys, values, bias_query, bias_value, doc_lengths, grad_out):
    x = lax.axis_index("xlo")
    y = lax.axis_index("y")
    core = lax.axis_index("core")
    width = GROUP * HEAD_DIM

    def by_core(mine, other):
        return jnp.concatenate(
            [jnp.where(core == 0, mine, other), jnp.where(core == 0, other, mine)], axis=0
        )

    def columns(array, which, size):
        return jnp.where(which == 0, array[:, :size], array[:, size:])

    value_rows = (values.astype(F32) + bias_value.astype(F32)[None, :]).astype(BF16)

    def kv_head(which):
        return jnp.concatenate(
            [columns(keys, which, HEAD_DIM), columns(value_rows, which, HEAD_DIM)], axis=1
        )

    kv_other = lax.ppermute(kv_head(1 - core), "core", SWAP)
    chip_kv = by_core(kv_head(core), kv_other)
    from_low = lax.ppermute(chip_kv, "xlo", [(0, 1)])
    two = jnp.stack([jnp.where(x == 0, chip_kv, from_low), chip_kv])
    gathered = lax.all_gather(two, "y", axis=0, tiled=False)

    q_other = lax.ppermute(columns(queries, 1 - core, width), "core", SWAP)
    g_other = lax.ppermute(columns(grad_out, 1 - core, width), "core", SWAP)
    place = jnp.stack([core, x * 8 + y]).astype(jnp.int32)
    att_own, att_send, gq_own, gq_send, dkv, bias_part = attention(
        place, doc_lengths, queries, grad_out, q_other, g_other, bias_query[None, :], gathered
    )

    reduced = lax.psum_scatter(dkv, "y", scatter_dimension=0, tiled=False)

    att_other = lax.ppermute(att_send, "core", SWAP)
    gq_other = lax.ppermute(gq_send, "core", SWAP)

    def side_by_side(mine, other):
        return jnp.concatenate(
            [jnp.where(core == 0, mine, other), jnp.where(core == 0, other, mine)], axis=1
        )

    attended = side_by_side(att_own, att_other)
    grad_queries = side_by_side(gq_own, gq_other)

    over_packs = jnp.sum(everyone(bias_part, ("z", "xhi", "xlo"), 32), axis=0)
    over_all = jnp.sum(everyone(over_packs, ("y", "core"), 16).reshape(8, 2, 8, HEAD_DIM), axis=0)
    grad_bias_query = over_all[:, :GROUP].reshape(HEADS * HEAD_DIM)
    grad_bias_value = over_all[:, GROUP].reshape(KV_HEADS * HEAD_DIM)

    from_high = lax.ppermute(reduced[0], "xlo", [(1, 0)])
    total = jnp.where(
        x == 0, (reduced[0].astype(F32) + from_high.astype(F32)).astype(BF16), reduced[1]
    )
    mine = jnp.where(core == 0, total[:TOK], total[TOK:])
    theirs = jnp.where(core == 0, total[TOK:], total[:TOK])
    other = lax.ppermute(theirs, "core", SWAP)
    grad_keys = side_by_side(mine[:, :HEAD_DIM], other[:, :HEAD_DIM])
    grad_values = side_by_side(mine[:, HEAD_DIM:], other[:, HEAD_DIM:])
    return attended, grad_queries, grad_keys, grad_values, grad_bias_query, grad_bias_value


def solution(mesh):
    parts = Mesh(mesh.devices.reshape(8, 2, 2, 8, 2), ("z", "xhi", "xlo", "y", "core"))
    rows = P(("z", "xhi") + SEQ, None)
    in_specs = (rows, rows, rows, P(), P(), P(("z", "xhi"), None), rows)
    out_specs = (rows, rows, rows, rows, P(), P())
    return jax.shard_map(body, mesh=parts, in_specs=in_specs, out_specs=out_specs, check_vma=False)
```

```python
import functools
import math

import jax
import jax.numpy as jnp
from jax import lax
from jax.experimental import pallas as pl
from jax.experimental.pallas import tpu as pltpu
from jax.sharding import Mesh, PartitionSpec as P

HEADS = 14
KV_HEADS = 2
HEAD_DIM = 128
GROUP = HEADS // KV_HEADS
TOK = 128
CHUNK = 256
LONGEST = 3072
SLOTS = LONGEST // CHUNK + 1
NDOC = 16
SCALE = 1.0 / math.sqrt(HEAD_DIM)
LOG2E = math.log2(math.e)
NEGATIVE = -1e30
F32 = jnp.float32
BF16 = jnp.bfloat16


def dot(a, b):
    return jnp.dot(a, b, preferred_element_type=F32)


def fold_rows(values, how):
    return how(values.reshape(values.shape[0] // 8, 8, values.shape[1]), axis=0)


def attention_kernel(
    place, lengths, q_own, g_own, q_other, g_other, bias_q, bias_v, kv,
    att_own, att_send, gq_own, gq_send, dkv, bias_out,
    q_s, qt_s, g_s, gt_s, v_s, s_s, p_s, d_s, mx_s, l_s, ot_s, dqt_s, rl_s, delta_s, mask_s, bv_s,
):
    core = place[0]
    chunk_id = place[1]
    first_token = chunk_id * CHUNK

    token = first_token + lax.broadcasted_iota(jnp.int32, (1, CHUNK), 1)
    first_seen = jnp.zeros((1, CHUNK), jnp.int32)
    begin = jnp.int32(0)
    lowest = jnp.int32(0)
    for i in range(NDOC):
        first_seen = jnp.where(token >= begin, begin, first_seen)
        lowest = jnp.where(first_token >= begin, begin, lowest)
        begin = begin + lengths[0, i]
    low = lax.div(lowest, jnp.int32(CHUNK))

    own_at = pl.multiple_of(core * TOK, TOK)
    other_at = pl.multiple_of((1 - core) * TOK, TOK)
    for h in range(GROUP):
        cols = pl.ds(h * HEAD_DIM, HEAD_DIM)
        own_cols = pl.ds(pl.multiple_of((core * GROUP + h) * HEAD_DIM, HEAD_DIM), HEAD_DIM)
        bias_row = bias_q[:, own_cols].astype(F32)
        own_rows = pl.ds(h * CHUNK + own_at, TOK)
        other_rows = pl.ds(h * CHUNK + other_at, TOK)
        q_s[own_rows, :] = (q_own[:, own_cols].astype(F32) + bias_row).astype(BF16)
        q_s[other_rows, :] = (q_other[:, cols].astype(F32) + bias_row).astype(BF16)
        g_s[own_rows, :] = g_own[:, own_cols]
        g_s[other_rows, :] = g_other[:, cols]
    for h in range(GROUP):
        at = pl.ds(h * CHUNK, CHUNK)
        qt_s[:, at] = q_s[at, :].T
        gt_s[:, at] = g_s[at, :].T
    mx_s[...] = jnp.full(mx_s.shape, NEGATIVE, F32)
    l_s[...] = jnp.zeros(l_s.shape, F32)
    ot_s[...] = jnp.zeros(ot_s.shape, F32)
    dqt_s[...] = jnp.zeros(dqt_s.shape, F32)
    bv_s[...] = jnp.zeros(bv_s.shape, F32)
    dkv[...] = jnp.zeros(dkv.shape, BF16)
    bias_v_row = bias_v[:, pl.ds(pl.multiple_of(core * HEAD_DIM, HEAD_DIM), HEAD_DIM)].astype(F32)

    def where_of(c):
        return lax.rem(c, 8), lax.div(c, 8)

    def scores(c, carry):
        y, x = where_of(c)
        keys = kv[y, x, :, :HEAD_DIM]
        v_s[c - low] = (kv[y, x, :, HEAD_DIM:].astype(F32) + bias_v_row).astype(BF16)
        key_index = c * CHUNK + lax.broadcasted_iota(jnp.int32, (CHUNK, CHUNK), 0)
        allowed = jnp.logical_and(key_index <= token, key_index >= first_seen)
        mask_s[...] = jnp.where(allowed, 0.0, NEGATIVE)
        for h in range(GROUP):
            at = pl.ds(h * CHUNK, CHUNK)
            raw = dot(keys, qt_s[:, at]) * (SCALE * LOG2E) + mask_s[...]
            s_s[c - low, :, at] = raw
            mx_s[:, at] = jnp.maximum(mx_s[:, at], fold_rows(raw, jnp.max))
        return carry

    lax.fori_loop(low, chunk_id + 1, scores, 0)
    mx_s[...] = jnp.broadcast_to(jnp.max(mx_s[...], axis=0, keepdims=True), mx_s.shape)

    def weigh(c, carry):
        values_t = v_s[c - low].T
        for h in range(GROUP):
            at = pl.ds(h * CHUNK, CHUNK)
            probs = jnp.exp2(s_s[c - low, :, at] - mx_s[0:1, at])
            s_s[c - low, :, at] = probs
            l_s[:, at] = l_s[:, at] + fold_rows(probs, jnp.sum)
            ot_s[:, at] = ot_s[:, at] + dot(values_t, probs.astype(BF16))
        return carry

    lax.fori_loop(low, chunk_id + 1, weigh, 0)

    for h in range(GROUP):
        at = pl.ds(h * CHUNK, CHUNK)
        cols = pl.ds(h * HEAD_DIM, HEAD_DIM)
        inverse = 1.0 / jnp.sum(l_s[:, at], axis=0, keepdims=True)
        rl_s[:, at] = jnp.broadcast_to(inverse, (8, CHUNK))
        out_t = (ot_s[:, at] * inverse).astype(BF16)
        delta = jnp.sum(out_t.astype(F32) * gt_s[:, at].astype(F32), axis=0, keepdims=True)
        delta_s[:, at] = jnp.broadcast_to(delta, (8, CHUNK))
        rows = out_t.T.reshape(2, TOK, HEAD_DIM)
        att_own[:, cols] = jnp.where(core == 0, rows[0], rows[1])
        att_send[:, cols] = jnp.where(core == 0, rows[1], rows[0])

    def slopes_of(c, carry):
        y, x = where_of(c)
        values = v_s[c - low]
        for h in range(GROUP):
            at = pl.ds(h * CHUNK, CHUNK)
            dots = dot(values, gt_s[:, at])
            probs = s_s[c - low, :, at] * rl_s[0:1, at]
            p_s[:, at] = probs.astype(BF16)
            d_s[:, at] = (probs * (dots - delta_s[0:1, at])).astype(BF16)
        dk = dot(d_s[...], q_s[...])
        dv = dot(p_s[...], g_s[...])
        keys_t = kv[y, x, :, :HEAD_DIM].T
        dqt_s[...] = dqt_s[...] + dot(keys_t, d_s[...])
        dkv[y, x, :, :HEAD_DIM] = (dk * SCALE).astype(BF16)
        dkv[y, x, :, HEAD_DIM:] = dv.astype(BF16)
        bv_s[...] = bv_s[...] + fold_rows(dv, jnp.sum)
        return carry

    lax.fori_loop(low, chunk_id + 1, slopes_of, 0)

    for h in range(GROUP):
        cols = pl.ds(h * HEAD_DIM, HEAD_DIM)
        grad = (dqt_s[:, pl.ds(h * CHUNK, CHUNK)] * SCALE).T
        bias_out[h : h + 1, :] = jnp.sum(grad, axis=0, keepdims=True)
        rows = grad.astype(BF16).reshape(2, TOK, HEAD_DIM)
        gq_own[:, cols] = jnp.where(core == 0, rows[0], rows[1])
        gq_send[:, cols] = jnp.where(core == 0, rows[1], rows[0])
    bias_out[GROUP : GROUP + 1, :] = jnp.sum(bv_s[...], axis=0, keepdims=True)


def attention(place, lengths, q_own, g_own, q_other, g_other, bias_q, bias_v, kv):
    half = jax.ShapeDtypeStruct((TOK, GROUP * HEAD_DIM), BF16)
    vmem = pl.BlockSpec(memory_space=pltpu.VMEM)
    smem = pl.BlockSpec(memory_space=pltpu.SMEM)
    queries = GROUP * CHUNK
    stat = pltpu.VMEM((8, queries), F32)
    pairs = CHUNK * SLOTS * queries
    return pl.pallas_call(
        attention_kernel,
        out_shape=[half] * 4
        + [
            jax.ShapeDtypeStruct(kv.shape, BF16),
            jax.ShapeDtypeStruct((8, HEAD_DIM), F32),
        ],
        in_specs=[smem] * 2 + [vmem] * 7,
        out_specs=[vmem] * 6,
        scratch_shapes=[
            pltpu.VMEM((queries, HEAD_DIM), BF16),
            pltpu.VMEM((HEAD_DIM, queries), BF16),
            pltpu.VMEM((queries, HEAD_DIM), BF16),
            pltpu.VMEM((HEAD_DIM, queries), BF16),
            pltpu.VMEM((SLOTS, CHUNK, HEAD_DIM), BF16),
            pltpu.VMEM((SLOTS, CHUNK, queries), F32),
            pltpu.VMEM((CHUNK, queries), BF16),
            pltpu.VMEM((CHUNK, queries), BF16),
            stat,
            stat,
            pltpu.VMEM((HEAD_DIM, queries), F32),
            pltpu.VMEM((HEAD_DIM, queries), F32),
            stat,
            stat,
            pltpu.VMEM((CHUNK, CHUNK), F32),
            pltpu.VMEM((8, HEAD_DIM), F32),
        ],
        compiler_params=pltpu.CompilerParams(vmem_limit_bytes=58 * 1024 * 1024),
        cost_estimate=pl.CostEstimate(
            flops=12 * pairs * HEAD_DIM, bytes_accessed=8 << 20, transcendentals=pairs
        ),
    )(place, lengths, q_own, g_own, q_other, g_other, bias_q, bias_v, kv)


SEQ = ("xlo", "y", "core")
SWAP = [(0, 1), (1, 0)]


def everyone(part, axes, count):
    spread = jnp.broadcast_to(part[None], (count,) + part.shape)
    return lax.all_to_all(spread, axes, split_axis=0, concat_axis=0, tiled=True)


def body(queries, keys, values, bias_query, bias_value, doc_lengths, grad_out):
    x = lax.axis_index("xlo")
    y = lax.axis_index("y")
    core = lax.axis_index("core")
    width = GROUP * HEAD_DIM
    low_core = core == 0

    def columns(array, which, size):
        return jnp.where(which == 0, array[:, :size], array[:, size:])

    def joined(mine, other, axis):
        return jnp.where(
            low_core,
            jnp.concatenate([mine, other], axis=axis),
            jnp.concatenate([other, mine], axis=axis),
        )

    def kv_head(which):
        return jnp.concatenate(
            [columns(keys, which, HEAD_DIM), columns(values, which, HEAD_DIM)], axis=1
        )

    kv_mine, kv_send = kv_head(core), kv_head(1 - core)
    kv_other = lax.ppermute(kv_send, "core", SWAP)
    low_mine = lax.ppermute(kv_mine, "xlo", [(0, 1)])
    low_other = lax.ppermute(kv_send, ("xlo", "core"), [(0, 3), (1, 2)])
    own = joined(kv_mine, kv_other, 0)
    two = jnp.stack([jnp.where(x == 0, own, joined(low_mine, low_other, 0)), own])
    gathered = lax.all_gather(two, "y", axis=0, tiled=False)

    q_other = lax.ppermute(columns(queries, 1 - core, width), "core", SWAP)
    g_other = lax.ppermute(columns(grad_out, 1 - core, width), "core", SWAP)
    place = jnp.stack([core, x * 8 + y]).astype(jnp.int32)
    att_own, att_send, gq_own, gq_send, dkv, bias_part = attention(
        place,
        doc_lengths,
        queries,
        grad_out,
        q_other,
        g_other,
        bias_query[None, :],
        bias_value[None, :],
        gathered,
    )

    reduced = lax.psum_scatter(dkv, "y", scatter_dimension=0, tiled=False)

    att_other = lax.ppermute(att_send, "core", SWAP)
    gq_other = lax.ppermute(gq_send, "core", SWAP)
    attended = joined(att_own, att_other, 1)
    grad_queries = joined(gq_own, gq_other, 1)
    over_packs = jnp.sum(everyone(bias_part, ("z", "xhi", "xlo"), 32), axis=0)
    over_all = jnp.sum(everyone(over_packs, ("y", "core"), 16).reshape(8, 2, 8, HEAD_DIM), axis=0)
    grad_bias_query = over_all[:, :GROUP].reshape(HEADS * HEAD_DIM)
    grad_bias_value = over_all[:, GROUP].reshape(KV_HEADS * HEAD_DIM)
    reduced, attended, grad_queries, grad_bias_query, grad_bias_value = lax.optimization_barrier(
        (reduced, attended, grad_queries, grad_bias_query, grad_bias_value)
    )

    low_sum = reduced[0]
    half_sum = jnp.where(x == 0, low_sum, reduced[1])

    def tokens(array, which):
        return jnp.where(which == 0, array[:TOK], array[TOK:])

    from_core = lax.ppermute(tokens(half_sum, 1 - core), "core", SWAP)
    high_mine = lax.ppermute(tokens(low_sum, core), "xlo", [(1, 0)])
    high_other = lax.ppermute(tokens(low_sum, 1 - core), ("xlo", "core"), [(2, 1), (3, 0)])

    def added(first, second):
        return (first.astype(F32) + jnp.where(x == 0, second.astype(F32), 0.0)).astype(BF16)

    mine = added(tokens(half_sum, core), high_mine)
    other = added(from_core, high_other)
    grad_keys = joined(mine[:, :HEAD_DIM], other[:, :HEAD_DIM], 1)
    grad_values = joined(mine[:, HEAD_DIM:], other[:, HEAD_DIM:], 1)
    return attended, grad_queries, grad_keys, grad_values, grad_bias_query, grad_bias_value


def solution(mesh):
    parts = Mesh(mesh.devices.reshape(8, 2, 2, 8, 2), ("z", "xhi", "xlo", "y", "core"))
    rows = P(("z", "xhi") + SEQ, None)
    in_specs = (rows, rows, rows, P(), P(), P(("z", "xhi"), None), rows)
    out_specs = (rows, rows, rows, rows, P(), P())
    return jax.shard_map(body, mesh=parts, in_specs=in_specs, out_specs=out_specs, check_vma=False)
```

```python
import functools
import math

import jax
import jax.numpy as jnp
from jax import lax
from jax.experimental import pallas as pl
from jax.experimental.pallas import tpu as pltpu
from jax.sharding import Mesh, PartitionSpec as P

HEADS = 14
KV_HEADS = 2
HEAD_DIM = 128
GROUP = HEADS // KV_HEADS
TOK = 128
CHUNK = 256
LONGEST = 3072
SLOTS = LONGEST // CHUNK + 1
NDOC = 16
SCALE = 1.0 / math.sqrt(HEAD_DIM)
LOG2E = math.log2(math.e)
NEGATIVE = -1e30
F32 = jnp.float32
BF16 = jnp.bfloat16


def dot(a, b):
    return jnp.dot(a, b, preferred_element_type=F32)


def fold_rows(values, how):
    return how(values.reshape(values.shape[0] // 8, 8, values.shape[1]), axis=0)


def arrange_kernel(place, q_own, g_own, q_other, g_other, bias_q, q_s, qt_s, g_s, gt_s):
    core = place[0]
    for h in range(GROUP):
        cols = pl.ds(h * HEAD_DIM, HEAD_DIM)
        own_cols = pl.ds(pl.multiple_of((core * GROUP + h) * HEAD_DIM, HEAD_DIM), HEAD_DIM)
        bias_row = bias_q[:, own_cols].astype(F32)
        own_rows = pl.ds(h * CHUNK, TOK)
        other_rows = pl.ds(h * CHUNK + TOK, TOK)
        q_s[own_rows, :] = (q_own[:, own_cols].astype(F32) + bias_row).astype(BF16)
        q_s[other_rows, :] = (q_other[:, cols].astype(F32) + bias_row).astype(BF16)
        g_s[own_rows, :] = g_own[:, own_cols]
        g_s[other_rows, :] = g_other[:, cols]
    for h in range(GROUP):
        at = pl.ds(h * CHUNK, CHUNK)
        qt_s[:, at] = q_s[at, :].T
        gt_s[:, at] = g_s[at, :].T


def arrange(place, q_own, g_own, q_other, g_other, bias_q):
    vmem = pl.BlockSpec(memory_space=pltpu.VMEM)
    smem = pl.BlockSpec(memory_space=pltpu.SMEM)
    rows = jax.ShapeDtypeStruct((GROUP * CHUNK, HEAD_DIM), BF16)
    columns = jax.ShapeDtypeStruct((HEAD_DIM, GROUP * CHUNK), BF16)
    return pl.pallas_call(
        arrange_kernel,
        out_shape=[rows, columns, rows, columns],
        in_specs=[smem] + [vmem] * 5,
        out_specs=[vmem] * 4,
        compiler_params=pltpu.CompilerParams(vmem_limit_bytes=24 * 1024 * 1024),
        cost_estimate=pl.CostEstimate(flops=1 << 22, bytes_accessed=4 << 20, transcendentals=0),
    )(place, q_own, g_own, q_other, g_other, bias_q)


def attention_kernel(
    place, lengths, q_s, qt_s, g_s, gt_s, bias_v, kv,
    att_own, att_send, gq_own, gq_send, dkv, bias_out,
    v_s, s_s, p_s, d_s, mx_s, l_s, ot_s, dqt_s, rl_s, delta_s, mask_s, bv_s,
):
    core = place[0]
    chunk_id = place[1]
    first_token = chunk_id * CHUNK
    half_start = chunk_id - lax.rem(chunk_id, 8)

    def position(shape, dim):
        return lax.rem(lax.broadcasted_iota(jnp.int32, shape, dim) + core * TOK, CHUNK)

    token = first_token + position((1, CHUNK), 1)
    first_seen = jnp.zeros((1, CHUNK), jnp.int32)
    begin = jnp.int32(0)
    lowest = jnp.int32(0)
    for i in range(NDOC):
        first_seen = jnp.where(token >= begin, begin, first_seen)
        lowest = jnp.where(first_token >= begin, begin, lowest)
        begin = begin + lengths[0, i]
    low = lax.div(lowest, jnp.int32(CHUNK))

    mx_s[...] = jnp.full(mx_s.shape, NEGATIVE, F32)
    l_s[...] = jnp.zeros(l_s.shape, F32)
    ot_s[...] = jnp.zeros(ot_s.shape, F32)
    dqt_s[...] = jnp.zeros(dqt_s.shape, F32)
    bv_s[...] = jnp.zeros(bv_s.shape, F32)
    dkv[...] = jnp.zeros(dkv.shape, BF16)
    bias_v_row = bias_v[:, pl.ds(pl.multiple_of(core * HEAD_DIM, HEAD_DIM), HEAD_DIM)].astype(F32)

    def rows_of(c):
        return lax.rem(c, 8), pl.ds(jnp.where(c >= half_start, 0, 2), 2)

    def part_of(c, at):
        y, blocks = rows_of(c)
        return kv[y, blocks, :, pl.ds(at, HEAD_DIM)].reshape(CHUNK, HEAD_DIM)

    count = chunk_id + 1 - low
    odd = lax.rem(count, 2)

    def scores(c, part):
        keys = part_of(c, 0)
        v_s[c - low] = (part_of(c, HEAD_DIM).astype(F32) + bias_v_row).astype(BF16)
        key_index = c * CHUNK + position((CHUNK, CHUNK), 0)
        allowed = jnp.logical_and(key_index <= token, key_index >= first_seen)
        mask_s[part] = jnp.where(allowed, 0.0, NEGATIVE)
        for h in range(GROUP):
            at = pl.ds(h * CHUNK, CHUNK)
            raw = dot(keys, qt_s[:, at]) * (SCALE * LOG2E) + mask_s[part]
            s_s[c - low, :, at] = raw
            mx_s[:, at] = jnp.maximum(mx_s[:, at], fold_rows(raw, jnp.max))

    def weigh(c, part):
        values_t = v_s[c - low].T
        for h in range(GROUP):
            at = pl.ds(h * CHUNK, CHUNK)
            probs = jnp.exp2(s_s[c - low, :, at] - mx_s[0:1, at])
            s_s[c - low, :, at] = probs
            l_s[:, at] = l_s[:, at] + fold_rows(probs, jnp.sum)
            ot_s[:, at] = ot_s[:, at] + dot(values_t, probs.astype(BF16))

    def in_pairs(step):
        @pl.when(odd == 1)
        def _():
            step(low, 0)

        def pair(i, carry):
            step(low + odd + 2 * i, 0)
            step(low + odd + 2 * i + 1, 1)
            return carry

        lax.fori_loop(0, lax.div(count, 2), pair, 0)

    in_pairs(scores)
    mx_s[...] = jnp.broadcast_to(jnp.max(mx_s[...], axis=0, keepdims=True), mx_s.shape)
    in_pairs(weigh)

    for h in range(GROUP):
        at = pl.ds(h * CHUNK, CHUNK)
        cols = pl.ds(h * HEAD_DIM, HEAD_DIM)
        inverse = 1.0 / jnp.sum(l_s[:, at], axis=0, keepdims=True)
        rl_s[:, at] = jnp.broadcast_to(inverse, (8, CHUNK))
        out_t = (ot_s[:, at] * inverse).astype(BF16)
        delta = jnp.sum(out_t.astype(F32) * gt_s[:, at].astype(F32), axis=0, keepdims=True)
        delta_s[:, at] = jnp.broadcast_to(delta, (8, CHUNK))
        rows = out_t.T
        att_own[:, cols] = rows[:TOK]
        att_send[:, cols] = rows[TOK:]

    def slopes_of(c, part):
        values = v_s[c - low]
        for h in range(GROUP):
            at = pl.ds(h * CHUNK, CHUNK)
            dots = dot(values, gt_s[:, at])
            probs = s_s[c - low, :, at] * rl_s[0:1, at]
            p_s[part, :, at] = probs.astype(BF16)
            d_s[part, :, at] = (probs * (dots - delta_s[0:1, at])).astype(BF16)

    def gradients(c, part):
        dk = dot(d_s[part], q_s[...])
        dv = dot(p_s[part], g_s[...])
        keys_t = part_of(c, 0).T
        dqt_s[...] = dqt_s[...] + dot(keys_t, d_s[part])
        y, blocks = rows_of(c)
        dkv[y, blocks, :, :HEAD_DIM] = (dk * SCALE).astype(BF16).reshape(2, TOK, HEAD_DIM)
        dkv[y, blocks, :, HEAD_DIM:] = dv.astype(BF16).reshape(2, TOK, HEAD_DIM)
        bv_s[...] = bv_s[...] + fold_rows(dv, jnp.sum)

    @pl.when(odd == 0)
    def _():
        slopes_of(low, 0)
        gradients(low, 0)

    first = low + 1 - odd
    slopes_of(first, 0)

    def staggered(i, carry):
        c = first + 2 * i
        slopes_of(c + 1, 1)
        gradients(c, 0)
        slopes_of(c + 2, 0)
        gradients(c + 1, 1)
        return carry

    lax.fori_loop(0, lax.div(chunk_id - first, 2), staggered, 0)
    gradients(chunk_id, 0)

    for h in range(GROUP):
        cols = pl.ds(h * HEAD_DIM, HEAD_DIM)
        grad = (dqt_s[:, pl.ds(h * CHUNK, CHUNK)] * SCALE).T
        bias_out[h : h + 1, :] = jnp.sum(grad, axis=0, keepdims=True)
        rows = grad.astype(BF16)
        gq_own[:, cols] = rows[:TOK]
        gq_send[:, cols] = rows[TOK:]
    bias_out[GROUP : GROUP + 1, :] = jnp.sum(bv_s[...], axis=0, keepdims=True)


def attention(place, lengths, q_rows, q_cols, g_rows, g_cols, bias_v, kv):
    half = jax.ShapeDtypeStruct((TOK, GROUP * HEAD_DIM), BF16)
    vmem = pl.BlockSpec(memory_space=pltpu.VMEM)
    smem = pl.BlockSpec(memory_space=pltpu.SMEM)
    queries = GROUP * CHUNK
    stat = pltpu.VMEM((8, queries), F32)
    pairs = CHUNK * SLOTS * queries
    return pl.pallas_call(
        attention_kernel,
        out_shape=[half] * 4
        + [
            jax.ShapeDtypeStruct(kv.shape, BF16),
            jax.ShapeDtypeStruct((8, HEAD_DIM), F32),
        ],
        in_specs=[smem] * 2 + [vmem] * 6,
        out_specs=[vmem] * 6,
        scratch_shapes=[
            pltpu.VMEM((SLOTS, CHUNK, HEAD_DIM), BF16),
            pltpu.VMEM((SLOTS, CHUNK, queries), F32),
            pltpu.VMEM((2, CHUNK, queries), BF16),
            pltpu.VMEM((2, CHUNK, queries), BF16),
            stat,
            stat,
            pltpu.VMEM((HEAD_DIM, queries), F32),
            pltpu.VMEM((HEAD_DIM, queries), F32),
            stat,
            stat,
            pltpu.VMEM((2, CHUNK, CHUNK), F32),
            pltpu.VMEM((8, HEAD_DIM), F32),
        ],
        compiler_params=pltpu.CompilerParams(vmem_limit_bytes=58 * 1024 * 1024),
        cost_estimate=pl.CostEstimate(
            flops=12 * pairs * HEAD_DIM, bytes_accessed=8 << 20, transcendentals=pairs
        ),
    )(place, lengths, q_rows, q_cols, g_rows, g_cols, bias_v, kv)


SEQ = ("xlo", "y", "core")
SWAP = [(0, 1), (1, 0)]


def everyone(part, axes, count):
    spread = jnp.broadcast_to(part[None], (count,) + part.shape)
    return lax.all_to_all(spread, axes, split_axis=0, concat_axis=0, tiled=True)


def body(queries, keys, values, bias_query, bias_value, doc_lengths, grad_out):
    x = lax.axis_index("xlo")
    y = lax.axis_index("y")
    core = lax.axis_index("core")
    width = GROUP * HEAD_DIM
    low_core = core == 0

    def columns(array, which, size):
        return jnp.where(which == 0, array[:, :size], array[:, size:])

    def joined(mine, other, axis):
        return jnp.where(
            low_core,
            jnp.concatenate([mine, other], axis=axis),
            jnp.concatenate([other, mine], axis=axis),
        )

    def kv_head(which):
        return jnp.concatenate(
            [columns(keys, which, HEAD_DIM), columns(values, which, HEAD_DIM)], axis=1
        )

    kv_mine, kv_send = kv_head(core), kv_head(1 - core)
    low_mine = lax.ppermute(kv_mine, "xlo", [(0, 1)])
    low_other = lax.ppermute(kv_send, ("xlo", "core"), [(0, 3), (1, 2)])
    kv_other = lax.ppermute(kv_send, "core", SWAP)
    gathered = lax.all_gather(
        jnp.stack([kv_mine, kv_other, low_mine, low_other]), "y", axis=0, tiled=False
    )

    place = jnp.stack([core, x * 8 + y]).astype(jnp.int32)
    q_other = lax.ppermute(columns(queries, 1 - core, width), "core", SWAP)
    g_other = lax.ppermute(columns(grad_out, 1 - core, width), "core", SWAP)
    arranged = arrange(place, queries, grad_out, q_other, g_other, bias_query[None, :])
    att_own, att_send, gq_own, gq_send, dkv, bias_part = attention(
        place, doc_lengths, *arranged, bias_value[None, :], gathered
    )

    reduced = lax.psum_scatter(dkv, "y", scatter_dimension=0, tiled=False)

    att_other = lax.ppermute(att_send, "core", SWAP)
    gq_other = lax.ppermute(gq_send, "core", SWAP)
    attended = joined(att_own, att_other, 1)
    grad_queries = joined(gq_own, gq_other, 1)
    over_packs = jnp.sum(everyone(bias_part, ("z", "xhi", "xlo"), 32), axis=0)
    over_all = jnp.sum(everyone(over_packs, ("y", "core"), 16).reshape(8, 2, 8, HEAD_DIM), axis=0)
    grad_bias_query = over_all[:, :GROUP].reshape(HEADS * HEAD_DIM)
    grad_bias_value = over_all[:, GROUP].reshape(KV_HEADS * HEAD_DIM)
    reduced, attended, grad_queries, grad_bias_query, grad_bias_value = lax.optimization_barrier(
        (reduced, attended, grad_queries, grad_bias_query, grad_bias_value)
    )

    high_mine = lax.ppermute(reduced[2], "xlo", [(1, 0)])
    high_other = lax.ppermute(reduced[3], ("xlo", "core"), [(2, 1), (3, 0)])
    from_core = lax.ppermute(reduced[1], "core", SWAP)
    mine = (reduced[0].astype(F32) + high_mine.astype(F32)).astype(BF16)
    other = (from_core.astype(F32) + high_other.astype(F32)).astype(BF16)
    grad_keys = joined(mine[:, :HEAD_DIM], other[:, :HEAD_DIM], 1)
    grad_values = joined(mine[:, HEAD_DIM:], other[:, HEAD_DIM:], 1)
    return attended, grad_queries, grad_keys, grad_values, grad_bias_query, grad_bias_value


def solution(mesh):
    parts = Mesh(mesh.devices.reshape(8, 2, 2, 8, 2), ("z", "xhi", "xlo", "y", "core"))
    rows = P(("z", "xhi") + SEQ, None)
    in_specs = (rows, rows, rows, P(), P(), P(("z", "xhi"), None), rows)
    out_specs = (rows, rows, rows, rows, P(), P())
    return jax.shard_map(body, mesh=parts, in_specs=in_specs, out_specs=out_specs, check_vma=False)
```

```python
import functools
import math

import jax
import jax.numpy as jnp
from jax import lax
from jax.experimental import pallas as pl
from jax.experimental.pallas import tpu as pltpu
from jax.sharding import Mesh, PartitionSpec as P

HEADS = 14
KV_HEADS = 2
HEAD_DIM = 128
GROUP = HEADS // KV_HEADS
TOK = 128
CHUNK = 256
LONGEST = 3072
SLOTS = LONGEST // CHUNK + 1
NDOC = 16
SCALE = 1.0 / math.sqrt(HEAD_DIM)
LOG2E = math.log2(math.e)
NEGATIVE = -1e30
F32 = jnp.float32
BF16 = jnp.bfloat16


def dot(a, b):
    return jnp.dot(a, b, preferred_element_type=F32)


def fold_rows(values, how):
    return how(values.reshape(values.shape[0] // 8, 8, values.shape[1]), axis=0)


def arrange_kernel(place, first, second, bias_q, q_s, qt_s, g_s, gt_s):
    head = place[0]
    width = GROUP * HEAD_DIM
    for h in range(GROUP):
        at = h * HEAD_DIM
        bias_row = bias_q[:, pl.ds(pl.multiple_of(head * width + at, HEAD_DIM), HEAD_DIM)].astype(F32)
        for part, rows in enumerate((first, second)):
            to = pl.ds(h * CHUNK + part * TOK, TOK)
            q_s[to, :] = (rows[:, pl.ds(at, HEAD_DIM)].astype(F32) + bias_row).astype(BF16)
            g_s[to, :] = rows[:, pl.ds(width + at, HEAD_DIM)]
    for h in range(GROUP):
        at = pl.ds(h * CHUNK, CHUNK)
        qt_s[:, at] = q_s[at, :].T
        gt_s[:, at] = g_s[at, :].T


def arrange(place, first, second, bias_q):
    vmem = pl.BlockSpec(memory_space=pltpu.VMEM)
    smem = pl.BlockSpec(memory_space=pltpu.SMEM)
    rows = jax.ShapeDtypeStruct((GROUP * CHUNK, HEAD_DIM), BF16)
    columns = jax.ShapeDtypeStruct((HEAD_DIM, GROUP * CHUNK), BF16)
    return pl.pallas_call(
        arrange_kernel,
        out_shape=[rows, columns, rows, columns],
        in_specs=[smem] + [vmem] * 3,
        out_specs=[vmem] * 4,
        compiler_params=pltpu.CompilerParams(vmem_limit_bytes=24 * 1024 * 1024),
        cost_estimate=pl.CostEstimate(flops=1 << 22, bytes_accessed=4 << 20, transcendentals=0),
    )(place, first, second, bias_q)


def attention_kernel(
    place, lengths, q_s, qt_s, g_s, gt_s, bias_v, kv_half, kv_low,
    first, second, dkv_half, dkv_low, bias_out,
    v_s, s_s, p_s, d_s, mx_s, l_s, ot_s, dqt_s, rl_s, delta_s, mask_s, bv_s,
):
    head = place[0]
    chunk_id = place[1]
    first_token = chunk_id * CHUNK
    half_start = chunk_id - lax.rem(chunk_id, 8)

    def position(shape, dim):
        return lax.rem(lax.broadcasted_iota(jnp.int32, shape, dim) + head * TOK, CHUNK)

    token = first_token + position((1, CHUNK), 1)
    first_seen = jnp.zeros((1, CHUNK), jnp.int32)
    begin = jnp.int32(0)
    lowest = jnp.int32(0)
    for i in range(NDOC):
        first_seen = jnp.where(token >= begin, begin, first_seen)
        lowest = jnp.where(first_token >= begin, begin, lowest)
        begin = begin + lengths[0, i]
    low = lax.div(lowest, jnp.int32(CHUNK))

    mx_s[...] = jnp.full(mx_s.shape, NEGATIVE, F32)
    l_s[...] = jnp.zeros(l_s.shape, F32)
    ot_s[...] = jnp.zeros(ot_s.shape, F32)
    dqt_s[...] = jnp.zeros(dqt_s.shape, F32)
    bv_s[...] = jnp.zeros(bv_s.shape, F32)
    dkv_half[...] = jnp.zeros(dkv_half.shape, BF16)
    dkv_low[...] = jnp.zeros(dkv_low.shape, BF16)
    bias_v_row = bias_v[:, pl.ds(pl.multiple_of(head * HEAD_DIM, HEAD_DIM), HEAD_DIM)].astype(F32)

    def part_of(c, at):
        y, cols = lax.rem(c, 8), pl.ds(at, HEAD_DIM)
        rows = jnp.where(c >= half_start, kv_half[y, :, :, cols], kv_low[y, :, :, cols])
        return rows.reshape(CHUNK, HEAD_DIM)

    count = chunk_id + 1 - low
    odd = lax.rem(count, 2)

    def scores(c, part):
        keys = part_of(c, 0)
        v_s[c - low] = (part_of(c, HEAD_DIM).astype(F32) + bias_v_row).astype(BF16)
        key_index = c * CHUNK + position((CHUNK, CHUNK), 0)
        allowed = jnp.logical_and(key_index <= token, key_index >= first_seen)
        mask_s[part] = jnp.where(allowed, 0.0, NEGATIVE)
        for h in range(GROUP):
            at = pl.ds(h * CHUNK, CHUNK)
            raw = dot(keys, qt_s[:, at]) * (SCALE * LOG2E) + mask_s[part]
            s_s[c - low, :, at] = raw
            mx_s[:, at] = jnp.maximum(mx_s[:, at], fold_rows(raw, jnp.max))

    def weigh(c, part):
        values_t = v_s[c - low].T
        for h in range(GROUP):
            at = pl.ds(h * CHUNK, CHUNK)
            probs = jnp.exp2(s_s[c - low, :, at] - mx_s[0:1, at])
            s_s[c - low, :, at] = probs
            l_s[:, at] = l_s[:, at] + fold_rows(probs, jnp.sum)
            ot_s[:, at] = ot_s[:, at] + dot(values_t, probs.astype(BF16))

    def in_pairs(step):
        @pl.when(odd == 1)
        def _():
            step(low, 0)

        def pair(i, carry):
            step(low + odd + 2 * i, 0)
            step(low + odd + 2 * i + 1, 1)
            return carry

        lax.fori_loop(0, lax.div(count, 2), pair, 0)

    in_pairs(scores)
    mx_s[...] = jnp.broadcast_to(jnp.max(mx_s[...], axis=0, keepdims=True), mx_s.shape)
    in_pairs(weigh)

    for h in range(GROUP):
        at = pl.ds(h * CHUNK, CHUNK)
        inverse = 1.0 / jnp.sum(l_s[:, at], axis=0, keepdims=True)
        rl_s[:, at] = jnp.broadcast_to(inverse, (8, CHUNK))
        out = (ot_s[:, at] * inverse).astype(BF16)
        cols = pl.ds(h * HEAD_DIM, HEAD_DIM)
        rows = out.T
        first[:, cols] = rows[:TOK]
        second[:, cols] = rows[TOK:]
        delta = jnp.sum(out.astype(F32) * gt_s[:, at].astype(F32), axis=0, keepdims=True)
        delta_s[:, at] = jnp.broadcast_to(delta, (8, CHUNK))

    def slopes_of(c, part):
        values = v_s[c - low]
        for h in range(GROUP):
            at = pl.ds(h * CHUNK, CHUNK)
            dots = dot(values, gt_s[:, at])
            probs = s_s[c - low, :, at] * rl_s[0:1, at]
            p_s[part, :, at] = probs.astype(BF16)
            d_s[part, :, at] = (probs * (dots - delta_s[0:1, at])).astype(BF16)

    def gradients(c, part):
        dk = dot(d_s[part], q_s[...])
        dv = dot(p_s[part], g_s[...])
        keys_t = part_of(c, 0).T
        dqt_s[...] = dqt_s[...] + dot(keys_t, d_s[part])
        bv_s[...] = bv_s[...] + fold_rows(dv, jnp.sum)
        y = lax.rem(c, 8)
        dk = (dk * SCALE).astype(BF16).reshape(2, TOK, HEAD_DIM)
        dv = dv.astype(BF16).reshape(2, TOK, HEAD_DIM)

        @pl.when(c >= half_start)
        def _():
            dkv_half[y, :, :, :HEAD_DIM] = dk
            dkv_half[y, :, :, HEAD_DIM:] = dv

        @pl.when(c < half_start)
        def _():
            dkv_low[y, :, :, :HEAD_DIM] = dk
            dkv_low[y, :, :, HEAD_DIM:] = dv

    @pl.when(odd == 0)
    def _():
        slopes_of(low, 0)
        gradients(low, 0)

    start = low + 1 - odd
    slopes_of(start, 0)

    def staggered(i, carry):
        c = start + 2 * i
        slopes_of(c + 1, 1)
        gradients(c, 0)
        slopes_of(c + 2, 0)
        gradients(c + 1, 1)
        return carry

    lax.fori_loop(0, lax.div(chunk_id - start, 2), staggered, 0)
    gradients(chunk_id, 0)

    for h in range(GROUP):
        grad = (dqt_s[:, pl.ds(h * CHUNK, CHUNK)] * SCALE).T
        bias_out[h : h + 1, :] = jnp.sum(grad, axis=0, keepdims=True)
        rows = grad.astype(BF16)
        cols = pl.ds((GROUP + h) * HEAD_DIM, HEAD_DIM)
        first[:, cols] = rows[:TOK]
        second[:, cols] = rows[TOK:]
    bias_out[GROUP : GROUP + 1, :] = jnp.sum(bv_s[...], axis=0, keepdims=True)


def attention(place, lengths, q_rows, q_cols, g_rows, g_cols, bias_v, kv_half, kv_low):
    vmem = pl.BlockSpec(memory_space=pltpu.VMEM)
    smem = pl.BlockSpec(memory_space=pltpu.SMEM)
    queries = GROUP * CHUNK
    stat = pltpu.VMEM((8, queries), F32)
    pairs = CHUNK * SLOTS * queries
    return pl.pallas_call(
        attention_kernel,
        out_shape=[
            jax.ShapeDtypeStruct((TOK, 2 * GROUP * HEAD_DIM), BF16),
            jax.ShapeDtypeStruct((TOK, 2 * GROUP * HEAD_DIM), BF16),
            jax.ShapeDtypeStruct(kv_half.shape, BF16),
            jax.ShapeDtypeStruct(kv_low.shape, BF16),
            jax.ShapeDtypeStruct((8, HEAD_DIM), F32),
        ],
        in_specs=[smem] * 2 + [vmem] * 7,
        out_specs=[vmem] * 5,
        scratch_shapes=[
            pltpu.VMEM((SLOTS, CHUNK, HEAD_DIM), BF16),
            pltpu.VMEM((SLOTS, CHUNK, queries), F32),
            pltpu.VMEM((2, CHUNK, queries), BF16),
            pltpu.VMEM((2, CHUNK, queries), BF16),
            stat,
            stat,
            pltpu.VMEM((HEAD_DIM, queries), F32),
            pltpu.VMEM((HEAD_DIM, queries), F32),
            stat,
            stat,
            pltpu.VMEM((2, CHUNK, CHUNK), F32),
            pltpu.VMEM((8, HEAD_DIM), F32),
        ],
        compiler_params=pltpu.CompilerParams(vmem_limit_bytes=39 * 1024 * 1024),
        cost_estimate=pl.CostEstimate(
            flops=12 * pairs * HEAD_DIM, bytes_accessed=8 << 20, transcendentals=pairs
        ),
    )(place, lengths, q_rows, q_cols, g_rows, g_cols, bias_v, kv_half, kv_low)


def merge_kernel(half, upper, bias_own, bias_other, out):
    sums = bias_own[...] + bias_other[...]
    high = sums.astype(BF16)
    rows = jnp.concatenate([high, (sums - high.astype(F32)).astype(BF16)], axis=1)
    rows = jnp.concatenate([rows, jnp.zeros_like(rows)], axis=0)
    for y in range(8):
        for part in range(2):
            total = half[y, part].astype(F32) + upper[y, part].astype(F32)
            out[y, part * TOK : (part + 1) * TOK, :] = total.astype(BF16)
        out[y, CHUNK:, :] = rows


def merge(half, upper, bias_own, bias_other):
    vmem = pl.BlockSpec(memory_space=pltpu.VMEM)
    return pl.pallas_call(
        merge_kernel,
        out_shape=jax.ShapeDtypeStruct((8, CHUNK + 16, 2 * HEAD_DIM), BF16),
        in_specs=[vmem] * 4,
        out_specs=vmem,
        compiler_params=pltpu.CompilerParams(vmem_limit_bytes=12 * 1024 * 1024),
        cost_estimate=pl.CostEstimate(flops=1 << 20, bytes_accessed=3 << 20, transcendentals=0),
    )(half, upper, bias_own, bias_other)


def reduce_kernel(got, first, second, bias_sum):
    for part, out in enumerate((first, second)):
        rows = pl.ds(part * TOK, TOK)
        total = got[0, rows, :].astype(F32)
        for y in range(1, 8):
            total = total + got[y, rows, :].astype(F32)
        out[...] = total.astype(BF16)
    total = got[0, CHUNK:, :].astype(F32)
    for y in range(1, 8):
        total = total + got[y, CHUNK:, :].astype(F32)
    bias_sum[...] = total[:8, :HEAD_DIM] + total[:8, HEAD_DIM:]


def reduce(got):
    vmem = pl.BlockSpec(memory_space=pltpu.VMEM)
    rows = jax.ShapeDtypeStruct((TOK, 2 * HEAD_DIM), BF16)
    return pl.pallas_call(
        reduce_kernel,
        out_shape=[rows] * 2 + [jax.ShapeDtypeStruct((8, HEAD_DIM), F32)],
        in_specs=[vmem],
        out_specs=[vmem] * 3,
        compiler_params=pltpu.CompilerParams(vmem_limit_bytes=12 * 1024 * 1024),
        cost_estimate=pl.CostEstimate(flops=1 << 20, bytes_accessed=1 << 20, transcendentals=0),
    )(got)


def combine_kernel(place, mine, other, gk, gv):
    core = place[2]
    own_cols = pl.ds(pl.multiple_of(core * HEAD_DIM, HEAD_DIM), HEAD_DIM)
    other_cols = pl.ds(pl.multiple_of((1 - core) * HEAD_DIM, HEAD_DIM), HEAD_DIM)
    gk[:, own_cols] = mine[:, :HEAD_DIM]
    gk[:, other_cols] = other[:, :HEAD_DIM]
    gv[:, own_cols] = mine[:, HEAD_DIM:]
    gv[:, other_cols] = other[:, HEAD_DIM:]


def combine(place, mine, other):
    rows = jax.ShapeDtypeStruct((TOK, KV_HEADS * HEAD_DIM), BF16)
    vmem = pl.BlockSpec(memory_space=pltpu.VMEM)
    smem = pl.BlockSpec(memory_space=pltpu.SMEM)
    return pl.pallas_call(
        combine_kernel,
        out_shape=[rows] * 2,
        in_specs=[smem] + [vmem] * 2,
        out_specs=[vmem] * 2,
        compiler_params=pltpu.CompilerParams(vmem_limit_bytes=8 * 1024 * 1024),
        cost_estimate=pl.CostEstimate(flops=1 << 17, bytes_accessed=1 << 19, transcendentals=0),
    )(place, mine, other)


SEQ = ("xlo", "y", "core")

QUAD = ("xlo", "core")
FIRST = [(0, 0), (1, 2), (2, 1), (3, 3)]
SECOND = [(0, 2), (1, 0), (2, 3), (3, 1)]
SECOND_BACK = [(b, a) for a, b in SECOND]


def everyone(part, axes, count):
    spread = jnp.broadcast_to(part[None], (count,) + part.shape)
    return lax.all_to_all(spread, axes, split_axis=0, concat_axis=0, tiled=True)


def body(queries, keys, values, bias_query, bias_value, doc_lengths, grad_out):
    x = lax.axis_index("xlo")
    y = lax.axis_index("y")
    core = lax.axis_index("core")
    width = GROUP * HEAD_DIM

    def columns(array, which, size):
        return jnp.where(which == 0, array[:, :size], array[:, size:])

    def joined(mine, other):
        return jnp.where(
            core == 0,
            jnp.concatenate([mine, other], axis=1),
            jnp.concatenate([other, mine], axis=1),
        )

    def head_of(first, second, which, size):
        return jnp.concatenate([columns(first, which, size), columns(second, which, size)], axis=1)

    kv_first = lax.ppermute(head_of(keys, values, core, HEAD_DIM), QUAD, FIRST)
    kv_second = lax.ppermute(head_of(keys, values, 1 - core, HEAD_DIM), QUAD, SECOND)
    kv_half = everyone(jnp.stack([kv_first, kv_second]), "y", 8)
    place = jnp.stack([x, core * 8 + y, core]).astype(jnp.int32)
    rows_first = lax.ppermute(head_of(queries, grad_out, core, width), QUAD, FIRST)
    rows_second = lax.ppermute(head_of(queries, grad_out, 1 - core, width), QUAD, SECOND)
    arranged = arrange(place, rows_first, rows_second, bias_query[None, :])
    kv_half, *arranged = lax.optimization_barrier((kv_half, *arranged))
    kv_low = lax.ppermute(kv_half, "core", [(0, 1)])
    back_first, back_second, dkv_half, dkv_low, bias_part = attention(
        place, doc_lengths, *arranged, bias_value[None, :], kv_half, kv_low
    )

    from_upper = lax.ppermute(dkv_low, "core", [(1, 0)])
    bias_other = lax.ppermute(bias_part, "core", [(0, 1), (1, 0)])
    terms = merge(dkv_half, from_upper, bias_part, bias_other)
    got = lax.all_to_all(terms, "y", split_axis=0, concat_axis=0, tiled=True)

    back_first = lax.ppermute(back_first, QUAD, FIRST)
    back_second = lax.ppermute(back_second, QUAD, SECOND_BACK)
    attended = joined(back_first[:, :width], back_second[:, :width])
    grad_queries = joined(back_first[:, width:], back_second[:, width:])
    got, attended, grad_queries = lax.optimization_barrier((got, attended, grad_queries))

    sum_first, sum_second, bias_sum = reduce(got)
    sum_first = lax.ppermute(sum_first, QUAD, FIRST)
    sum_second = lax.ppermute(sum_second, QUAD, SECOND_BACK)
    bias_all = everyone(bias_sum, ("z", "xhi", "xlo"), 32)
    bias_both = jnp.sum(bias_all.reshape(16, 2, 8, HEAD_DIM), axis=0)
    grad_bias_query = bias_both[:, :GROUP].reshape(HEADS * HEAD_DIM)
    grad_bias_value = bias_both[:, GROUP].reshape(KV_HEADS * HEAD_DIM)
    grad_keys, grad_values = combine(place, sum_first, sum_second)
    return attended, grad_queries, grad_keys, grad_values, grad_bias_query, grad_bias_value


def solution(mesh):
    parts = Mesh(mesh.devices.reshape(8, 2, 2, 8, 2), ("z", "xhi", "xlo", "y", "core"))
    rows = P(("z", "xhi") + SEQ, None)
    in_specs = (rows, rows, rows, P(), P(), P(("z", "xhi"), None), rows)
    out_specs = (rows, rows, rows, rows, P(), P())
    return jax.shard_map(body, mesh=parts, in_specs=in_specs, out_specs=out_specs, check_vma=False)
```

```python
import functools
import math

import jax
import jax.numpy as jnp
from jax import lax
from jax.experimental import pallas as pl
from jax.experimental.pallas import tpu as pltpu
from jax.sharding import Mesh, PartitionSpec as P

HEADS = 14
KV_HEADS = 2
HEAD_DIM = 128
GROUP = HEADS // KV_HEADS
TOK = 128
CHUNK = 256
LONGEST = 3072
SLOTS = LONGEST // CHUNK + 1
NDOC = 16
SCALE = 1.0 / math.sqrt(HEAD_DIM)
LOG2E = math.log2(math.e)
NEGATIVE = -1e30
F32 = jnp.float32
BF16 = jnp.bfloat16


def dot(a, b):
    return jnp.dot(a, b, preferred_element_type=F32)


def fold_rows(values, how):
    return how(values.reshape(values.shape[0] // 8, 8, values.shape[1]), axis=0)


def arrange_kernel(place, first, second, bias_q, q_s, qt_s, g_s, gt_s):
    head = place[0]
    width = GROUP * HEAD_DIM
    for h in range(GROUP):
        at = h * HEAD_DIM
        bias_row = bias_q[:, pl.ds(pl.multiple_of(head * width + at, HEAD_DIM), HEAD_DIM)].astype(F32)
        for part, rows in enumerate((first, second)):
            to = pl.ds(h * CHUNK + part * TOK, TOK)
            q_s[to, :] = (rows[:, pl.ds(at, HEAD_DIM)].astype(F32) + bias_row).astype(BF16)
            g_s[to, :] = rows[:, pl.ds(width + at, HEAD_DIM)]
    for h in range(GROUP):
        at = pl.ds(h * CHUNK, CHUNK)
        qt_s[:, at] = q_s[at, :].T
        gt_s[:, at] = g_s[at, :].T


def arrange(place, first, second, bias_q):
    vmem = pl.BlockSpec(memory_space=pltpu.VMEM)
    smem = pl.BlockSpec(memory_space=pltpu.SMEM)
    rows = jax.ShapeDtypeStruct((GROUP * CHUNK, HEAD_DIM), BF16)
    columns = jax.ShapeDtypeStruct((HEAD_DIM, GROUP * CHUNK), BF16)
    return pl.pallas_call(
        arrange_kernel,
        out_shape=[rows, columns, rows, columns],
        in_specs=[smem] + [vmem] * 3,
        out_specs=[vmem] * 4,
        compiler_params=pltpu.CompilerParams(vmem_limit_bytes=24 * 1024 * 1024),
        cost_estimate=pl.CostEstimate(flops=1 << 22, bytes_accessed=4 << 20, transcendentals=0),
    )(place, first, second, bias_q)


def attention_kernel(
    place, lengths, q_s, qt_s, g_s, gt_s, bias_v, kv_half, kv_low,
    first, second, dkv_half, dkv_low, bias_out,
    v_s, s_s, p_s, d_s, mx_s, l_s, ot_s, dqt_s, rl_s, delta_s, mask_s, bv_s,
):
    head = place[0]
    chunk_id = place[1]
    first_token = chunk_id * CHUNK
    half_start = chunk_id - lax.rem(chunk_id, 8)

    def position(shape, dim):
        return lax.rem(lax.broadcasted_iota(jnp.int32, shape, dim) + head * TOK, CHUNK)

    token = first_token + position((1, CHUNK), 1)
    first_seen = jnp.zeros((1, CHUNK), jnp.int32)
    begin = jnp.int32(0)
    lowest = jnp.int32(0)
    for i in range(NDOC):
        first_seen = jnp.where(token >= begin, begin, first_seen)
        lowest = jnp.where(first_token >= begin, begin, lowest)
        begin = begin + lengths[0, i]
    low = lax.div(lowest, jnp.int32(CHUNK))

    mx_s[...] = jnp.full(mx_s.shape, NEGATIVE, F32)
    l_s[...] = jnp.zeros(l_s.shape, F32)
    ot_s[...] = jnp.zeros(ot_s.shape, F32)
    dqt_s[...] = jnp.zeros(dqt_s.shape, F32)
    bv_s[...] = jnp.zeros(bv_s.shape, F32)
    dkv_half[...] = jnp.zeros(dkv_half.shape, BF16)
    dkv_low[...] = jnp.zeros(dkv_low.shape, BF16)
    bias_v_row = bias_v[:, pl.ds(pl.multiple_of(head * HEAD_DIM, HEAD_DIM), HEAD_DIM)].astype(F32)

    def part_of(c, at):
        y, cols = lax.rem(c, 8), pl.ds(at, HEAD_DIM)
        rows = jnp.where(c >= half_start, kv_half[y, :, :, cols], kv_low[y, :, :, cols])
        return rows.reshape(CHUNK, HEAD_DIM)

    count = chunk_id + 1 - low
    odd = lax.rem(count, 2)

    def scores(c, part):
        keys = part_of(c, 0)
        v_s[c - low] = (part_of(c, HEAD_DIM).astype(F32) + bias_v_row).astype(BF16)
        key_index = c * CHUNK + position((CHUNK, CHUNK), 0)
        allowed = jnp.logical_and(key_index <= token, key_index >= first_seen)
        mask_s[part] = jnp.where(allowed, 0.0, NEGATIVE)
        for h in range(GROUP):
            at = pl.ds(h * CHUNK, CHUNK)
            raw = dot(keys, qt_s[:, at]) * (SCALE * LOG2E) + mask_s[part]
            s_s[c - low, :, at] = raw
            mx_s[:, at] = jnp.maximum(mx_s[:, at], fold_rows(raw, jnp.max))

    def weigh(c, part):
        values_t = v_s[c - low].T
        for h in range(GROUP):
            at = pl.ds(h * CHUNK, CHUNK)
            probs = jnp.exp2(s_s[c - low, :, at] - mx_s[0:1, at])
            s_s[c - low, :, at] = probs
            l_s[:, at] = l_s[:, at] + fold_rows(probs, jnp.sum)
            ot_s[:, at] = ot_s[:, at] + dot(values_t, probs.astype(BF16))

    def in_pairs(step):
        @pl.when(odd == 1)
        def _():
            step(low, 0)

        def pair(i, carry):
            step(low + odd + 2 * i, 0)
            step(low + odd + 2 * i + 1, 1)
            return carry

        lax.fori_loop(0, lax.div(count, 2), pair, 0)

    in_pairs(scores)
    mx_s[...] = jnp.broadcast_to(jnp.max(mx_s[...], axis=0, keepdims=True), mx_s.shape)
    in_pairs(weigh)

    for h in range(GROUP):
        at = pl.ds(h * CHUNK, CHUNK)
        inverse = 1.0 / jnp.sum(l_s[:, at], axis=0, keepdims=True)
        rl_s[:, at] = jnp.broadcast_to(inverse, (8, CHUNK))
        out = (ot_s[:, at] * inverse).astype(BF16)
        cols = pl.ds(h * HEAD_DIM, HEAD_DIM)
        rows = out.T
        first[:, cols] = rows[:TOK]
        second[:, cols] = rows[TOK:]
        delta = jnp.sum(out.astype(F32) * gt_s[:, at].astype(F32), axis=0, keepdims=True)
        delta_s[:, at] = jnp.broadcast_to(delta, (8, CHUNK))

    def slopes_of(c, part):
        values = v_s[c - low]
        for h in range(GROUP):
            at = pl.ds(h * CHUNK, CHUNK)
            dots = dot(values, gt_s[:, at])
            probs = s_s[c - low, :, at] * rl_s[0:1, at]
            p_s[part, :, at] = probs.astype(BF16)
            d_s[part, :, at] = (probs * (dots - delta_s[0:1, at])).astype(BF16)

    def gradients(c, part):
        dk = dot(d_s[part], q_s[...])
        dv = dot(p_s[part], g_s[...])
        keys_t = part_of(c, 0).T
        dqt_s[...] = dqt_s[...] + dot(keys_t, d_s[part])
        bv_s[...] = bv_s[...] + fold_rows(dv, jnp.sum)
        y = lax.rem(c, 8)
        dk = (dk * SCALE).astype(BF16).reshape(2, TOK, HEAD_DIM)
        dv = dv.astype(BF16).reshape(2, TOK, HEAD_DIM)

        @pl.when(c >= half_start)
        def _():
            dkv_half[y, :, :, :HEAD_DIM] = dk
            dkv_half[y, :, :, HEAD_DIM:] = dv

        @pl.when(c < half_start)
        def _():
            dkv_low[y, :, :, :HEAD_DIM] = dk
            dkv_low[y, :, :, HEAD_DIM:] = dv

    @pl.when(odd == 0)
    def _():
        slopes_of(low, 0)
        gradients(low, 0)

    start = low + 1 - odd
    slopes_of(start, 0)

    def staggered(i, carry):
        c = start + 2 * i
        slopes_of(c + 1, 1)
        gradients(c, 0)
        slopes_of(c + 2, 0)
        gradients(c + 1, 1)
        return carry

    lax.fori_loop(0, lax.div(chunk_id - start, 2), staggered, 0)
    gradients(chunk_id, 0)

    for h in range(GROUP):
        grad = (dqt_s[:, pl.ds(h * CHUNK, CHUNK)] * SCALE).T
        bias_out[h : h + 1, :] = jnp.sum(grad, axis=0, keepdims=True)
        rows = grad.astype(BF16)
        cols = pl.ds((GROUP + h) * HEAD_DIM, HEAD_DIM)
        first[:, cols] = rows[:TOK]
        second[:, cols] = rows[TOK:]
    bias_out[GROUP : GROUP + 1, :] = jnp.sum(bv_s[...], axis=0, keepdims=True)


def attention(place, lengths, q_rows, q_cols, g_rows, g_cols, bias_v, kv_half, kv_low):
    vmem = pl.BlockSpec(memory_space=pltpu.VMEM)
    smem = pl.BlockSpec(memory_space=pltpu.SMEM)
    queries = GROUP * CHUNK
    stat = pltpu.VMEM((8, queries), F32)
    pairs = CHUNK * SLOTS * queries
    return pl.pallas_call(
        attention_kernel,
        out_shape=[
            jax.ShapeDtypeStruct((TOK, 2 * GROUP * HEAD_DIM), BF16),
            jax.ShapeDtypeStruct((TOK, 2 * GROUP * HEAD_DIM), BF16),
            jax.ShapeDtypeStruct(kv_half.shape, BF16),
            jax.ShapeDtypeStruct(kv_low.shape, BF16),
            jax.ShapeDtypeStruct((8, HEAD_DIM), F32),
        ],
        in_specs=[smem] * 2 + [vmem] * 7,
        out_specs=[vmem] * 5,
        scratch_shapes=[
            pltpu.VMEM((SLOTS, CHUNK, HEAD_DIM), BF16),
            pltpu.VMEM((SLOTS, CHUNK, queries), F32),
            pltpu.VMEM((2, CHUNK, queries), BF16),
            pltpu.VMEM((2, CHUNK, queries), BF16),
            stat,
            stat,
            pltpu.VMEM((HEAD_DIM, queries), F32),
            pltpu.VMEM((HEAD_DIM, queries), F32),
            stat,
            stat,
            pltpu.VMEM((2, CHUNK, CHUNK), F32),
            pltpu.VMEM((8, HEAD_DIM), F32),
        ],
        compiler_params=pltpu.CompilerParams(vmem_limit_bytes=39 * 1024 * 1024),
        cost_estimate=pl.CostEstimate(
            flops=12 * pairs * HEAD_DIM, bytes_accessed=8 << 20, transcendentals=pairs
        ),
    )(place, lengths, q_rows, q_cols, g_rows, g_cols, bias_v, kv_half, kv_low)


def merge_kernel(half, upper, out):
    for y in range(8):
        for part in range(2):
            total = half[y, part].astype(F32) + upper[y, part].astype(F32)
            out[y, part] = total.astype(BF16)


def merge(half, upper):
    vmem = pl.BlockSpec(memory_space=pltpu.VMEM)
    return pl.pallas_call(
        merge_kernel,
        out_shape=jax.ShapeDtypeStruct(half.shape, BF16),
        in_specs=[vmem] * 2,
        out_specs=vmem,
        compiler_params=pltpu.CompilerParams(vmem_limit_bytes=12 * 1024 * 1024),
        cost_estimate=pl.CostEstimate(flops=1 << 20, bytes_accessed=3 << 20, transcendentals=0),
    )(half, upper)


def reduce_kernel(got, first, second):
    for part, out in enumerate((first, second)):
        total = got[0, part].astype(F32)
        for y in range(1, 8):
            total = total + got[y, part].astype(F32)
        out[...] = total.astype(BF16)


def reduce(got):
    vmem = pl.BlockSpec(memory_space=pltpu.VMEM)
    rows = jax.ShapeDtypeStruct((TOK, 2 * HEAD_DIM), BF16)
    return pl.pallas_call(
        reduce_kernel,
        out_shape=[rows] * 2,
        in_specs=[vmem],
        out_specs=[vmem] * 2,
        compiler_params=pltpu.CompilerParams(vmem_limit_bytes=12 * 1024 * 1024),
        cost_estimate=pl.CostEstimate(flops=1 << 20, bytes_accessed=1 << 20, transcendentals=0),
    )(got)


def combine_kernel(place, mine, other, bias_sums, gk, gv, gbq, gbv):
    core = place[2]
    own_cols = pl.ds(pl.multiple_of(core * HEAD_DIM, HEAD_DIM), HEAD_DIM)
    other_cols = pl.ds(pl.multiple_of((1 - core) * HEAD_DIM, HEAD_DIM), HEAD_DIM)
    gk[:, own_cols] = mine[:, :HEAD_DIM]
    gk[:, other_cols] = other[:, :HEAD_DIM]
    gv[:, own_cols] = mine[:, HEAD_DIM:]
    gv[:, other_cols] = other[:, HEAD_DIM:]
    for head in range(KV_HEADS):
        total = bias_sums[8 * head]
        for y in range(1, 8):
            total = total + bias_sums[8 * head + y]
        for h in range(GROUP):
            gbq[pl.ds((head * GROUP + h) * HEAD_DIM, HEAD_DIM)] = total[h]
        gbv[pl.ds(head * HEAD_DIM, HEAD_DIM)] = total[GROUP]


def combine(place, mine, other, bias_sums):
    rows = jax.ShapeDtypeStruct((TOK, KV_HEADS * HEAD_DIM), BF16)
    vmem = pl.BlockSpec(memory_space=pltpu.VMEM)
    smem = pl.BlockSpec(memory_space=pltpu.SMEM)
    return pl.pallas_call(
        combine_kernel,
        out_shape=[rows] * 2
        + [jax.ShapeDtypeStruct((n * HEAD_DIM,), F32) for n in (HEADS, KV_HEADS)],
        in_specs=[smem] + [vmem] * 3,
        out_specs=[vmem] * 4,
        compiler_params=pltpu.CompilerParams(vmem_limit_bytes=8 * 1024 * 1024),
        cost_estimate=pl.CostEstimate(flops=1 << 17, bytes_accessed=1 << 19, transcendentals=0),
    )(place, mine, other, bias_sums)


SEQ = ("xlo", "y", "core")

QUAD = ("xlo", "core")
FIRST = [(0, 0), (1, 2), (2, 1), (3, 3)]
SECOND = [(0, 2), (1, 0), (2, 3), (3, 1)]
SECOND_BACK = [(b, a) for a, b in SECOND]


def everyone(part, axes, count):
    spread = jnp.broadcast_to(part[None], (count,) + part.shape)
    return lax.all_to_all(spread, axes, split_axis=0, concat_axis=0, tiled=True)


def body(queries, keys, values, bias_query, bias_value, doc_lengths, grad_out):
    x = lax.axis_index("xlo")
    y = lax.axis_index("y")
    core = lax.axis_index("core")
    width = GROUP * HEAD_DIM

    def columns(array, which, size):
        return jnp.where(which == 0, array[:, :size], array[:, size:])

    def joined(mine, other):
        return jnp.where(
            core == 0,
            jnp.concatenate([mine, other], axis=1),
            jnp.concatenate([other, mine], axis=1),
        )

    def head_of(first, second, which, size):
        return jnp.concatenate([columns(first, which, size), columns(second, which, size)], axis=1)

    kv_first = lax.ppermute(head_of(keys, values, core, HEAD_DIM), QUAD, FIRST)
    kv_second = lax.ppermute(head_of(keys, values, 1 - core, HEAD_DIM), QUAD, SECOND)
    kv_half = everyone(jnp.stack([kv_first, kv_second]), "y", 8)
    place = jnp.stack([x, core * 8 + y, core]).astype(jnp.int32)
    rows_first = lax.ppermute(head_of(queries, grad_out, core, width), QUAD, FIRST)
    rows_second = lax.ppermute(head_of(queries, grad_out, 1 - core, width), QUAD, SECOND)
    kv_half, rows_first, rows_second = lax.optimization_barrier((kv_half, rows_first, rows_second))
    kv_low = lax.ppermute(kv_half, "core", [(0, 1)])
    arranged = arrange(place, rows_first, rows_second, bias_query[None, :])
    back_first, back_second, dkv_half, dkv_low, bias_part = attention(
        place, doc_lengths, *arranged, bias_value[None, :], kv_half, kv_low
    )

    from_upper = lax.ppermute(dkv_low, "core", [(1, 0)])
    bias_sum = bias_part + lax.ppermute(bias_part, "core", [(0, 1), (1, 0)])
    dkv_half, from_upper, bias_sum = lax.optimization_barrier((dkv_half, from_upper, bias_sum))
    terms = merge(dkv_half, from_upper)
    got = lax.all_to_all(terms, "y", split_axis=0, concat_axis=0, tiled=True)

    back_first = lax.ppermute(back_first, QUAD, FIRST)
    back_second = lax.ppermute(back_second, QUAD, SECOND_BACK)
    attended = joined(back_first[:, :width], back_second[:, :width])
    grad_queries = joined(back_first[:, width:], back_second[:, width:])
    for axis, size, step in (("z", 8, 1), ("z", 8, 2), ("z", 8, 4)):
        bias_sum = bias_sum + lax.ppermute(bias_sum, axis, [(i, i ^ step) for i in range(size)])
    got, attended, grad_queries, bias_sum = lax.optimization_barrier(
        (got, attended, grad_queries, bias_sum)
    )

    sum_first, sum_second = reduce(got)
    sum_first = lax.ppermute(sum_first, QUAD, FIRST)
    sum_second = lax.ppermute(sum_second, QUAD, SECOND_BACK)
    bias_sum = bias_sum + lax.ppermute(bias_sum, "xhi", [(0, 1), (1, 0)])
    bias_sum, sum_first, sum_second = lax.optimization_barrier((bias_sum, sum_first, sum_second))
    bias_sums = everyone(bias_sum, ("xlo", "y"), 16)
    grad_keys, grad_values, grad_bias_query, grad_bias_value = combine(
        place, sum_first, sum_second, bias_sums
    )
    return attended, grad_queries, grad_keys, grad_values, grad_bias_query, grad_bias_value


def solution(mesh):
    parts = Mesh(mesh.devices.reshape(8, 2, 2, 8, 2), ("z", "xhi", "xlo", "y", "core"))
    rows = P(("z", "xhi") + SEQ, None)
    in_specs = (rows, rows, rows, P(), P(), P(("z", "xhi"), None), rows)
    out_specs = (rows, rows, rows, rows, P(), P())
    return jax.shard_map(body, mesh=parts, in_specs=in_specs, out_specs=out_specs, check_vma=False)
```
